512 devices in a mesh: pipe: 8 (over y), dp: 16 (over x, z_lo), tensor: 4 (over z_hi, core).
Axes of the slice: x: 4, y: 8, z: 8 (z_hi: 2, z_lo: 4; z = z_hi * 4 + z_lo), core: 2. Of those that a mesh axis runs over, the one named last changes fastest.
Arguments:
- handed: bfloat16 [8, 3584, 8192], P('pipe', 'dp', 'tensor'), may hold values from -6 to 6
- cotangent: bfloat16 [8, 3584, 512], P('pipe', 'dp', 'tensor'), may hold values from -6 to 6
- base_weight: bfloat16 [8, 8192, 512], P('pipe', 'tensor'), may hold values from -0.0625 to 0.0625
- adapt_down: bfloat16 [8, 16, 8192, 128], P('pipe', 'dp', 'tensor'), may hold values from -0.0625 to 0.0625
- adapt_up: bfloat16 [8, 16, 128, 512], P('pipe', 'dp', None, 'tensor'), may hold values from -0.5 to 0.5
- row_jobs: int32 [8, 3584, 1], P('pipe', 'dp'), may hold values from 0 to 15; in each aligned block of 224 rows (0 to 223, 224 to 447, ..., all dimensions but the last counted through in order) at most 32 rows name the same one
- job_ranks: int32 [16], replicated, may hold values from 16 to 128
Outputs:
- projected: bfloat16 [8, 3584, 512], P('pipe', 'dp', 'tensor')
- input_grad: bfloat16 [8, 3584, 8192], P('pipe', 'dp', 'tensor')
- down_gradient: bfloat16 [8, 16, 8192, 128], P('pipe', 'dp', 'tensor')
- up_gradient: bfloat16 [8, 16, 128, 512], P('pipe', 'dp', None, 'tensor')
The draws below stay inside these ranges and needn't reach their ends.
Inputs may be any that keep to these rules, and one draw needn't show every extreme that they name: `row_jobs`: within the rows of one device (aligned blocks of 224 rows) no job appears more than 32 times.
All inputs are finite; a program needn't handle non-finite values.
Results may differ from the reference program's by a relative error of at most 0.0049.
Values may be sent and summed in bfloat16 or wider, within the bound.
A program may use at most 64 MiB of HBM per device.

```python
import math
import jax
import jax.numpy as jnp
import numpy as np
from jax import lax

D = 8192
OUT = 512
RANK_PADDED = 128
ROWS_DEV = 224
JOBS = 16
CAP = 32
TOKENS = 3584
N_PIPE = 8
N_DP = 16


def with_ends(drawn, own_key, low, largest):
    place = [jax.random.randint(jax.random.fold_in(own_key, axis), (), 0, length) for axis, length in enumerate(drawn.shape)]
    main_axis = drawn.shape.index(max(drawn.shape))
    neighbour = place[:main_axis] + [(place[main_axis] + 1) % drawn.shape[main_axis]] + place[main_axis + 1:]
    return drawn.at[tuple(place)].set(low).at[tuple(neighbour)].set(largest)


def level_of(rng, extent, pieces, least, high):
    level, own = 1.0, jax.random.fold_in(rng, 6)
    for position, parts in pieces:
        steps = jnp.exp(jax.random.uniform(jax.random.fold_in(own, position), (parts,), jnp.float32, least / len(pieces), high / len(pieces)))
        level = level * jnp.repeat(steps, extent[position] // parts).reshape([-1 if axis == position else 1 for axis in range(len(extent))])
    return level


def deal_out(own_key, own, number, rows, number_of, top, bound, lean):
    ranking = jax.random.permutation(own_key, number_of)
    heavy_load, ordinary = load_shares(number_of, rows * top, bound, lean, True), load_shares(number_of, rows * top, bound, lean, False)
    places = jnp.arange(number_of)

    def named(lengths, offset_by):
        used = int((lengths > 0).sum())
        fixed = max(1, used // 4)
        moved = fixed + (places - fixed + offset_by * (used - fixed)) % max(1, number_of - fixed)
        return jnp.zeros((number_of,), jnp.int32).at[ranking[jnp.where(places < fixed, places, moved)]].set(jnp.asarray(lengths, jnp.int32))

    lengths = jnp.where(number % 4 == 0, named(heavy_load, number // 4), named(ordinary, number - number // 4 - 1))
    mixed = jax.random.permutation(jax.random.fold_in(own, 3), number_of)
    source_of, receiver = mixed[0:number_of // 2 * 2:2], mixed[1:number_of // 2 * 2:2]
    slack = jnp.minimum(lengths[source_of] - 1, bound - lengths[receiver]) // 2
    slack = jnp.where((source_of == ranking[0]) | (receiver == ranking[0]) | (lengths[receiver] == 0), 0, jnp.maximum(slack, 0))
    moved = jax.random.randint(jax.random.fold_in(own, 4), (number_of // 2,), 0, 1 << 20) % (slack + 1)
    lengths = lengths.at[source_of].add(-moved).at[receiver].add(moved)
    members = jnp.searchsorted(jnp.cumsum(lengths), jnp.arange(rows * top), side="right").astype(jnp.int32)
    grid = members.reshape(top, rows).T
    grid = grid[jax.random.permutation(jax.random.fold_in(own, 1), rows)]
    offset_by = jax.random.randint(jax.random.fold_in(own, 2), (rows, 1), 0, top)
    return jnp.take_along_axis(grid, (jnp.arange(top)[None, :] + offset_by) % top, axis=1)


def load_shares(amount, total, bound, slope, full):
    weights = [(1 << 20) // math.isqrt(rank ** slope) + 1 for rank in range(1, amount + 1)]
    largest = bound if full else min(bound, max(-(-total // amount), total * weights[0] // sum(weights)))
    least = 1 if total - largest >= amount - 1 else 0
    given, rest = [largest] + [least] * (amount - 1), total - largest - least * (amount - 1)
    while rest > 0:
        movable = [i for i in range(1, amount) if given[i] < largest] or [i for i in range(1, amount) if given[i] < bound]
        mass, remaining = sum([weights[i] for i in movable]), rest
        for i in movable:
            extra = min(bound - given[i], max(1, remaining * weights[i] // mass), rest)
            given[i] = given[i] + extra
            rest = rest - extra
    return np.array(given)


def normal_values(own_key, dims, scale, bound, cuts=(), kind=jnp.bfloat16):
    drawn = scale * jax.random.normal(own_key, dims, jnp.float32)
    if cuts:
        drawn = drawn * level_of(own_key, dims, cuts, -0.22, 0.18)
    return jnp.clip(drawn, -bound, bound).astype(kind)


def setup_inputs(seed: int = 0) -> dict:
    seeds = jax.random.split(jax.random.key(seed), 8)
    handed = normal_values(seeds[0], (N_PIPE, TOKENS, D), 1.0, 6.0, ((0, 8), (1, 16), (2, 4)))
    cotangent = normal_values(seeds[1], (N_PIPE, TOKENS, OUT), 1.0, 6.0, ((0, 8), (1, 16), (2, 4)))
    base_weight = normal_values(seeds[2], (N_PIPE, D, OUT), D ** -0.5, 0.0625, ((0, 8), (1, 4)))
    adapt_down = normal_values(seeds[3], (N_PIPE, JOBS, D, RANK_PADDED), D ** -0.5, 0.0625, ((0, 8), (1, 16), (2, 4)))
    adapt_up = normal_values(seeds[4], (N_PIPE, JOBS, RANK_PADDED, OUT), RANK_PADDED ** -0.5, 0.5, ((0, 8), (1, 16), (3, 4)))
    row_jobs_keys = jax.random.split(jax.random.fold_in(seeds[5], 1), N_PIPE * TOKENS // ROWS_DEV)
    row_jobs_turns = jax.random.permutation(jax.random.fold_in(seeds[5], 3), N_PIPE * TOKENS // ROWS_DEV)
    row_jobs = jax.vmap(lambda own, number: deal_out(jax.random.fold_in(seeds[5], 2), own, number, ROWS_DEV, JOBS, 1, CAP, 2))(row_jobs_keys, row_jobs_turns).reshape((N_PIPE, TOKENS, 1))
    job_ranks = with_ends(jax.random.randint(seeds[6], (JOBS,), RANK_PADDED // 8, RANK_PADDED + 1), jax.random.fold_in(seeds[6], 1), RANK_PADDED // 8, RANK_PADDED).astype(jnp.int32)
    return {"handed": handed, "cotangent": cotangent, "base_weight": base_weight, "adapt_down": adapt_down, "adapt_up": adapt_up, "row_jobs": row_jobs, "job_ranks": job_ranks}


adapter_alpha = 4.0

def one_section(inputs, grads_out, weight, down_factors, up_factors, row_ids, job_ranks):
    base_out = jnp.dot(inputs, weight, preferred_element_type=jnp.float32)
    frozen_backward = jnp.dot(grads_out, weight.T, preferred_element_type=jnp.float32)
    count_of_tokens = inputs.shape[0]
    count_of_jobs = down_factors.shape[0]
    most_rows = N_DP * CAP
    onehot = (row_ids[:, None] == jnp.arange(count_of_jobs, dtype=jnp.int32)[None, :]).astype(jnp.int32)
    counts = lax.optimization_barrier(jnp.sum(onehot, 0)).astype(jnp.int32)
    starts = (jnp.cumsum(counts) - counts).astype(jnp.int32)
    sorted_rows = jnp.argsort(row_ids, stable=True).astype(jnp.int32)
    padded = jnp.concatenate([sorted_rows, jnp.zeros((most_rows,), jnp.int32)])

    def job_split(index_of_job):
        selected_rows = lax.dynamic_slice(padded, (starts[index_of_job],), (most_rows,))
        live_mask = jnp.arange(most_rows, dtype=jnp.int32) < counts[index_of_job]
        rows_in = jnp.where(live_mask[:, None], inputs[selected_rows], jnp.zeros((), inputs.dtype))
        rows_grad = jnp.where(live_mask[:, None], grads_out[selected_rows], jnp.zeros((), grads_out.dtype))
        adapter_rank = job_ranks[index_of_job]
        scale_factor = adapter_alpha / jnp.sqrt(adapter_rank.astype(jnp.float32)) * (jnp.arange(RANK_PADDED, dtype=jnp.int32) < adapter_rank).astype(jnp.float32)
        reduced_state = (jnp.dot(rows_in, down_factors[index_of_job], preferred_element_type=jnp.float32) * scale_factor).astype(jnp.bfloat16)
        reduced_gradient = (jnp.dot(rows_grad, up_factors[index_of_job].T, preferred_element_type=jnp.float32) * scale_factor).astype(jnp.bfloat16)
        adapter_output = jnp.dot(reduced_state, up_factors[index_of_job], preferred_element_type=jnp.float32).astype(jnp.bfloat16)
        adapter_backward = jnp.dot(reduced_gradient, down_factors[index_of_job].T, preferred_element_type=jnp.float32).astype(jnp.bfloat16)
        down_gradient = jnp.dot(rows_in.T, reduced_gradient, preferred_element_type=jnp.float32).astype(jnp.bfloat16)
        up_gradient = jnp.dot(reduced_state.T, rows_grad, preferred_element_type=jnp.float32).astype(jnp.bfloat16)
        return (selected_rows, live_mask, adapter_output, adapter_backward, down_gradient, up_gradient)
    selected_rows, live_mask, adapter_output, adapter_backward, down_gradient, up_gradient = lax.map(job_split, jnp.arange(count_of_jobs, dtype=jnp.int32))
    flattened_rows = selected_rows.reshape(-1)
    flattened_live = live_mask.reshape(-1)[:, None]
    output_sum = jnp.zeros((count_of_tokens, up_factors.shape[2]), jnp.float32).at[flattened_rows].add(jnp.where(flattened_live, adapter_output.reshape(-1, up_factors.shape[2]).astype(jnp.float32), jnp.zeros((), jnp.float32)))
    backward_sum = jnp.zeros((count_of_tokens, down_factors.shape[1]), jnp.float32).at[flattened_rows].add(jnp.where(flattened_live, adapter_backward.reshape(-1, down_factors.shape[1]).astype(jnp.float32), jnp.zeros((), jnp.float32)))
    projected = (base_out + output_sum).astype(jnp.bfloat16)
    incoming_gradient = (frozen_backward + backward_sum).astype(jnp.bfloat16)
    return (projected, incoming_gradient, down_gradient, up_gradient)

def reference(handed, cotangent, base_weight, adapt_down, adapt_up, row_jobs, job_ranks):
    incoming = jnp.roll(handed, 1, axis=0)

    def section_at(section_index):
        return one_section(incoming[section_index], cotangent[section_index], base_weight[section_index], adapt_down[section_index], adapt_up[section_index], row_jobs[section_index, :, 0], job_ranks)
    projected, incoming_gradient, down_gradient, up_gradient = lax.map(section_at, jnp.arange(N_PIPE, dtype=jnp.int32))
    return (projected, jnp.roll(incoming_gradient, -1, axis=0), down_gradient, up_gradient)
```

```python
import functools

import jax
import jax.numpy as jnp
from jax import lax
from jax.experimental import pallas as pl
from jax.experimental.pallas import tpu as pltpu
from jax.sharding import PartitionSpec as P

ALPHA = 4.0
NX = 4
NZ = 4
CAP = 32
NF = 8
ND = 4
RS0 = 3
XB = 6
YB = 9
LOW = XB + NF - 1
STEPS = LOW + 5
f32, bf16 = jnp.float32, jnp.bfloat16


def nn(a, b):
    return jnp.dot(a, b, preferred_element_type=f32)


def nt(a, b):
    return lax.dot_general(a, b, (((1,), (1,)), ((), ())), preferred_element_type=f32)


def tn(a, b):
    return lax.dot_general(a, b, (((0,), (0,)), ((), ())), preferred_element_type=f32)


def body(
    handed, cot, weight, down, up, jobs, ranks,
    proj, igrad, dgrad, ugrad,
    inp, to_slots, to_rows, xs, xr, cs, cr, cotf, up4, dn4,
    lgp, lgx, lgs, lgz, lg, lgt,
    lwp, lwx, lws, lwz, lw,
    bo, box, bos, boz, base,
    bs, br, los, lor, ybs,
    own, sp, rl, rr, ugs, ugr,
    y_s, y_r, x_s, x_r, c_s, c_r, ct_s, ct_r, up_s, up_r, dn_s, dn_r,
    ex_s, ex_r, b_s, b_r, lo_s, lo_r, yb_s, yb_r, rs_s, rl_r, rr_r, ug_s, ug_r,
):
    rows = inp.shape[1]
    fc = inp.shape[2]
    dc = dn4.shape[1] // ND
    wide = up.shape[3]
    npipe = lax.axis_size("pipe")
    p, d, t = lax.axis_index("pipe"), lax.axis_index("dp"), lax.axis_index("tensor")
    x, z = d // NZ, d % NZ
    c = t % 2
    h = t // 2
    after = {"pipe": (p + 1) % npipe}
    before = {"pipe": (p + npipe - 1) % npipe}
    x_peer = [{"dp": ((x + i) % NX) * NZ + z} for i in range(1, NX)]
    z_peer = [{"dp": x * NZ + (z + i) % NZ} for i in range(1, NZ)]
    z_up = {"dp": x * NZ + jnp.minimum(z + 1, NZ - 1)}
    z_dn = {"dp": x * NZ + jnp.maximum(z - 1, 0)}
    twin = {"tensor": t + 1 - 2 * c}
    far = {"tensor": (t + 2) % 4}

    def remote(src, dst, s, r, who):
        return pltpu.make_async_remote_copy(
            src_ref=src, dst_ref=dst, send_sem=s, recv_sem=r,
            device_id=who, device_id_type=pl.DeviceIdType.MESH,
        )

    bar = pltpu.get_barrier_semaphore()
    everyone = [after, before, twin, far] + x_peer + z_peer
    for who in everyone:
        pl.semaphore_signal(bar, inc=1, device_id=who, device_id_type=pl.DeviceIdType.MESH)

    mine = jobs[0]
    lanes = lax.broadcasted_iota(jnp.int32, (rows, 128), 1)
    hot = (mine == lanes).astype(f32).astype(bf16)
    same = nt(hot, hot)
    i0 = lax.broadcasted_iota(jnp.int32, (rows, rows), 0)
    i1 = lax.broadcasted_iota(jnp.int32, (rows, rows), 1)
    rank_col = jnp.sum(jnp.where(i1 < i0, same, 0.0), axis=1, keepdims=True)
    rank_row = jnp.sum(jnp.where(i0 < i1, same, 0.0), axis=0, keepdims=True)
    slot_col = mine.astype(f32) * CAP + rank_col
    numbers = lax.broadcasted_iota(jnp.int32, (16, 128), 1).astype(f32).astype(bf16)
    slot_row = nt(numbers, hot)[0:1] * CAP + rank_row
    slots = to_slots.shape[0]
    to_rows[...] = (
        lax.broadcasted_iota(jnp.int32, (rows, slots), 1).astype(f32) == slot_col
    ).astype(f32).astype(bf16)
    to_slots[...] = (
        lax.broadcasted_iota(jnp.int32, (slots, rows), 0).astype(f32) == slot_row
    ).astype(f32).astype(bf16)

    def y_copy(f):
        return remote(
            handed.at[0, :, pl.ds(pl.multiple_of(f * fc, fc), fc)], inp.at[f],
            y_s.at[f], y_r.at[f], after,
        )

    def c_copy(i):
        return remote(
            cs.at[(x + i) % NX], cr.at[:, x], c_s.at[i - 1], c_r.at[i - 1], x_peer[i - 1]
        )

    def x_copy(f, i):
        return remote(
            xs.at[f, (x + i) % NX], xr.at[f, :, x], x_s.at[f, i - 1], x_r.at[f, i - 1],
            x_peer[i - 1],
        )

    def b_copy(f, i):
        return remote(
            bs.at[f, :, (x + i) % NX], br.at[f, x], b_s.at[f, i - 1], b_r.at[f, i - 1],
            x_peer[i - 1],
        )

    def lo_copy(i):
        return remote(
            los.at[:, (x + i) % NX], lor.at[x], lo_s.at[i - 1], lo_r.at[i - 1],
            x_peer[i - 1],
        )

    def up_copy(i):
        return remote(up.at[0, 0], up4.at[z], up_s.at[i - 1], up_r.at[i - 1], z_peer[i - 1])

    def ug_copy(i):
        return remote(
            ugs.at[(z + i) % NZ], ugr.at[z], ug_s.at[i - 1], ug_r.at[i - 1], z_peer[i - 1]
        )

    lanes_of = lambda k: cotf.at[:, pl.ds(pl.multiple_of(k * wide, wide), wide)]
    cot_twin = remote(cot.at[0], lanes_of(t), ct_s.at[0], ct_r.at[0], twin)
    cot_far = remote(cot.at[0], lanes_of(t), ct_s.at[1], ct_r.at[1], far)
    cot_on = remote(
        lanes_of((t + 2) % 4), lanes_of((t + 2) % 4), ct_s.at[2], ct_r.at[2], twin
    )

    def dn_part(o, f):
        return dn4.at[o, pl.ds(pl.multiple_of(f * dc, dc), dc)]

    def own_dn(f, way):
        who, k = (z_up, 0) if way > 0 else (z_dn, 1)
        src = down.at[0, 0, pl.ds(pl.multiple_of(f * dc, dc), dc)]
        return remote(src, dn_part(z, f), dn_s.at[z, f, k], dn_r.at[z, f], who)

    def next_dn(o, f, way):
        who, k = (z_up, 0) if way > 0 else (z_dn, 1)
        return remote(dn_part(o, f), dn_part(o, f), dn_s.at[o, f, k], dn_r.at[o, f], who)

    half = lg.shape[0] // 2
    here, there = pl.multiple_of(c * half, half), pl.multiple_of((1 - c) * half, half)
    lg_twin = remote(lgp.at[pl.ds(there, half)], lgx, ex_s.at[0], ex_r.at[0], twin)
    lg_far = remote(lgs, lgz, ex_s.at[1], ex_r.at[1], far)
    lg_swap = remote(
        lg.at[pl.ds(here, half)], lg.at[pl.ds(here, half)], ex_s.at[2], ex_r.at[2], twin
    )
    lw_twin = remote(lwp.at[pl.ds(there, half)], lwx, ex_s.at[3], ex_r.at[3], twin)
    lw_far = remote(lws, lwz, ex_s.at[4], ex_r.at[4], far)
    lw_swap = remote(
        lw.at[pl.ds(here, half)], lw.at[pl.ds(here, half)], ex_s.at[5], ex_r.at[5], twin
    )
    bo_twin = remote(bo.at[1 - c], box, ex_s.at[6], ex_r.at[6], twin)
    bo_far = remote(bos, boz, ex_s.at[7], ex_r.at[7], far)

    def yb_copy(f):
        return remote(
            ybs.at[f], igrad.at[0, :, pl.ds(pl.multiple_of(f * fc, fc), fc)],
            yb_s.at[f], yb_r.at[f], before,
        )

    def rs_up(o, f):
        return remote(sp.at[o, f], rl.at[o, f], rs_s.at[o, f], rl_r.at[o, f], z_up)

    def rs_dn(o, f):
        return remote(sp.at[o, f], rr.at[o, f], rs_s.at[o, f], rr_r.at[o, f], z_dn)

    def each(count, fn):
        def go(i, carry):
            fn(i)
            return carry

        lax.fori_loop(0, count, go, 0)

    pl.semaphore_wait(bar, len(everyone))

    cot_twin.start()
    cot_far.start()
    for i in range(1, NZ):
        up_copy(i).start()
    y_copy(0).start()
    y_copy(1).start()
    for j in range(NX):
        got = nn(to_slots[j * 128 : (j + 1) * 128], cot[0]).astype(bf16)
        cs[j] = got.reshape(NZ, CAP, wide)
    for i in range(1, NX):
        c_copy(i).start()
    for k in range(NZ):
        cr[k, x] = cs[x, k]
    each(NF - 2, lambda f: y_copy(f + 2).start())

    @pl.when(z == 0)
    def _():
        each(ND, lambda f: own_dn(f, 1).start())

    @pl.when(z == NZ - 1)
    def _():
        each(ND, lambda f: own_dn(f, -1).start())

    up4[z] = up[0, 0]
    dn4[z] = down[0, 0]
    cotf[:, pl.ds(pl.multiple_of(t * wide, wide), wide)] = cot[0]
    bo[...] = jnp.zeros_like(bo)
    lwp[...] = jnp.zeros_like(lwp)

    def factor_of(k):
        rank = ranks[x * NZ + k]
        lane = lax.broadcasted_iota(jnp.int32, (1, 128), 1)
        many = jnp.full((1, 128), rank, jnp.int32)
        return jnp.where(lane < many, ALPHA / jnp.sqrt(many.astype(f32)), 0.0)

    def step(s, carry):
        @pl.when(s < NF)
        def _():
            f = s
            y_copy(f).wait_recv()
            block = inp[f]
            for j in range(NX):
                got = nn(to_slots[j * 128 : (j + 1) * 128], block).astype(bf16)
                xs[f, j] = got.reshape(NZ, CAP, fc)
            for i in range(1, NX):
                x_copy(f, i).start()
            for k in range(NZ):
                xr[f, k, x] = xs[f, x, k]
            part = nn(block, weight[0, pl.ds(pl.multiple_of(f * fc, fc), fc)])
            for k in range(4):
                bo[k % 2, k // 2] += part[:, k * wide : (k + 1) * wide]

        @pl.when((s % 3 == 0) & (s < 3 * ND))
        def _():
            @pl.when((z > 0) & (z < NZ - 1))
            def _():
                own_dn(s // 3, 1).start()
                own_dn(s // 3, -1).start()

        for o in range(NZ):
            dist = jnp.abs(z - o)
            g = s - dist
            f = g // 3

            @pl.when((dist > 0) & (g >= 0) & (g % 3 == 0) & (g < 3 * ND))
            def _():
                next_dn(o, f, 1).wait_recv()

                @pl.when((z > o) & (z < NZ - 1))
                def _():
                    next_dn(o, f, 1).start()

                @pl.when((z < o) & (z > 0))
                def _():
                    next_dn(o, f, -1).start()

        @pl.when(s == 0)
        def _():
            cot_far.wait_recv()
            cot_on.start()
            for i in range(1, NX):
                c_copy(i).wait_recv()
            for i in range(1, NZ):
                up_copy(i).wait_recv()
            for k in range(NZ):
                lgp[k * 128 : (k + 1) * 128] = nt(cr[k].reshape(128, wide), up4[k])
            lg_twin.start()

        @pl.when(s == 1)
        def _():
            lg_twin.wait_recv()
            lgx[...] += lgp[pl.ds(here, half)]
            lgs[...] = lgx[...].astype(lgs.dtype)
            lg_far.start()

        @pl.when(s == 2)
        def _():
            lg_far.wait_recv()
            total = lgx[...] + lgz[...].astype(f32)
            for k in range(2):
                lg[pl.ds(pl.multiple_of(c * half + k * 128, 128), 128)] = (
                    total[k * 128 : (k + 1) * 128] * factor_of(2 * c + k)
                ).astype(bf16)
            lg_swap.start()
            cot_twin.wait_recv()
            cot_on.wait_recv()

        @pl.when(s == RS0)
        def _():
            lg_swap.wait_recv()
            for k in range(NZ):
                lgt[k] = lg[k * 128 : (k + 1) * 128].T

        @pl.when((s >= RS0) & (s < RS0 + NF))
        def _():
            f = s - RS0
            for i in range(1, NX):
                x_copy(f, i).wait_recv()
            for k in range(NZ):
                own[k, f] = nn(lgt[k], xr[f, k].reshape(128, fc))

        fu = s - RS0 - z

        @pl.when((fu >= 0) & (fu < NF))
        def _():
            for o in range(1, NZ):

                @pl.when((o > z) & (z == 0))
                def _():
                    sp[o, fu] = own[o, fu].astype(bf16)
                    rs_up(o, fu).start()

                @pl.when((o > z) & (z > 0))
                def _():
                    rs_up(o, fu).wait_recv()
                    sp[o, fu] = (own[o, fu] + rl[o, fu].astype(f32)).astype(bf16)
                    rs_up(o, fu).start()

        fd = s - RS0 - (NZ - 1 - z)

        @pl.when((fd >= 0) & (fd < NF))
        def _():
            for o in range(NZ - 1):

                @pl.when((o < z) & (z == NZ - 1))
                def _():
                    sp[o, fd] = own[o, fd].astype(bf16)
                    rs_dn(o, fd).start()

                @pl.when((o < z) & (z < NZ - 1))
                def _():
                    rs_dn(o, fd).wait_recv()
                    sp[o, fd] = (own[o, fd] + rr[o, fd].astype(f32)).astype(bf16)
                    rs_dn(o, fd).start()

        fe = s - RS0 - (NZ - 1)

        @pl.when((fe >= 0) & (fe < NF))
        def _():
            @pl.when(z > 0)
            def _():
                rs_up(z, fe).wait_recv()
                own[z, fe] += rl[z, fe].astype(f32)

            @pl.when(z < NZ - 1)
            def _():
                rs_dn(z, fe).wait_recv()
                own[z, fe] += rr[z, fe].astype(f32)

            dgrad[0, 0, pl.ds(pl.multiple_of(fe * fc, fc), fc)] = own[z, fe].T.astype(bf16)

        @pl.when((s >= XB) & (s < XB + NF))
        def _():
            f = s - XB
            at = pl.ds(pl.multiple_of(f * fc, fc), fc)
            for k in range(NZ):
                back = nt(lg[k * 128 : (k + 1) * 128], dn4[k, at]).astype(bf16)
                bs[f, k] = back.reshape(NX, CAP, fc)
            for i in range(1, NX):
                b_copy(f, i).start()
            for k in range(NZ):
                br[f, x, k] = bs[f, k, x]
                lwp[k * 128 : (k + 1) * 128] += nn(xr[f, k].reshape(128, fc), dn4[k, at])

        @pl.when(s == NF)
        def _():
            bo_twin.start()

        @pl.when(s == NF + 1)
        def _():
            bo_twin.wait_recv()
            base[...] = bo[c, h] + box[h]
            bos[...] = (bo[c, 1 - h] + box[1 - h]).astype(bos.dtype)
            bo_far.start()

        @pl.when(s == NF + 3)
        def _():
            bo_far.wait_recv()
            base[...] += boz[...].astype(f32)

        @pl.when((s >= YB) & (s < YB + NF))
        def _():
            f = s - YB
            part = nt(cotf[...], weight[0, pl.ds(pl.multiple_of(f * fc, fc), fc)])
            for i in range(1, NX):
                b_copy(f, i).wait_recv()
            ybs[f] = (part + nn(to_rows[...], br[f].reshape(slots, fc))).astype(bf16)
            yb_copy(f).start()

        @pl.when(s == LOW)
        def _():
            lw_twin.start()

        @pl.when(s == LOW + 1)
        def _():
            lw_twin.wait_recv()
            lwx[...] += lwp[pl.ds(here, half)]
            lws[...] = lwx[...].astype(lws.dtype)
            lw_far.start()

        @pl.when(s == LOW + 2)
        def _():
            lw_far.wait_recv()
            total = lwx[...] + lwz[...].astype(f32)
            for k in range(2):
                lw[pl.ds(pl.multiple_of(c * half + k * 128, 128), 128)] = (
                    total[k * 128 : (k + 1) * 128] * factor_of(2 * c + k)
                ).astype(bf16)
            lw_swap.start()

        @pl.when(s == LOW + 3)
        def _():
            lw_swap.wait_recv()
            for k in range(NZ):
                low = lw[k * 128 : (k + 1) * 128]
                los[k] = nn(low, up4[k]).astype(bf16).reshape(NX, CAP, wide)
                ugs[k] = tn(low, cr[k].reshape(128, wide)).astype(bf16)
            for i in range(1, NX):
                lo_copy(i).start()
            for i in range(1, NZ):
                ug_copy(i).start()
            for k in range(NZ):
                lor[x, k] = los[k, x]

        @pl.when(s == LOW + 4)
        def _():
            for i in range(1, NX):
                lo_copy(i).wait_recv()
            proj[0] = (base[...] + nn(to_rows[...], lor[...].reshape(slots, wide))).astype(
                bf16
            )
            ugr[z] = ugs[z]
            for i in range(1, NZ):
                ug_copy(i).wait_recv()
            total = ugr[0].astype(f32)
            for k in range(1, NZ):
                total += ugr[k].astype(f32)
            ugrad[0, 0] = total.astype(bf16)

        return carry

    lax.fori_loop(0, STEPS, step, 0)

    for one in (cot_twin, cot_far, cot_on, lg_twin, lg_far, lg_swap, lw_twin, lw_far,
                lw_swap, bo_twin, bo_far):
        one.wait_send()
    for i in range(1, NX):
        c_copy(i).wait_send()
        lo_copy(i).wait_send()
    for i in range(1, NZ):
        up_copy(i).wait_send()
        ug_copy(i).wait_send()

    def last(f):
        y_copy(f).wait_send()
        for i in range(1, NX):
            x_copy(f, i).wait_send()
            b_copy(f, i).wait_send()
        yb_copy(f).wait_send()
        for o in range(NZ):

            @pl.when(o > z)
            def _():
                rs_up(o, f).wait_send()

            @pl.when(o < z)
            def _():
                rs_dn(o, f).wait_send()

    each(NF, last)

    def last_dn(f):
        for o in range(NZ):

            @pl.when((o <= z) & (z < NZ - 1))
            def _():
                next_dn(o, f, 1).wait_send()

            @pl.when((o >= z) & (z > 0))
            def _():
                next_dn(o, f, -1).wait_send()

    each(ND, last_dn)
    each(NF, lambda f: yb_copy(f).wait_recv())


def shards(handed, cotangent, base_weight, adapt_down, adapt_up, row_jobs, job_ranks):
    _, rows, feats = handed.shape
    wide = cotangent.shape[2]
    out = base_weight.shape[2]
    rank = adapt_down.shape[3]
    fc = feats // NF
    slots = NX * NZ * CAP
    lane = NX * CAP
    half = slots // 2
    v = pltpu.VMEM
    dma = pltpu.SemaphoreType.DMA
    scratch = [
        v((NF, rows, fc), bf16),
        v((slots, rows), bf16),
        v((rows, slots), bf16),
        v((NF, NX, NZ, CAP, fc), bf16),
        v((NF, NZ, NX, CAP, fc), bf16),
        v((NX, NZ, CAP, wide), bf16),
        v((NZ, NX, CAP, wide), bf16),
        v((rows, out), bf16),
        v((NZ, rank, wide), bf16),
        v((NZ, feats, rank), bf16),
        v((slots, rank), f32),
        v((half, rank), f32),
        v((half, rank), bf16),
        v((half, rank), bf16),
        v((slots, rank), bf16),
        v((NZ, rank, lane), bf16),
        v((slots, rank), f32),
        v((half, rank), f32),
        v((half, rank), bf16),
        v((half, rank), bf16),
        v((slots, rank), bf16),
        v((2, 2, rows, wide), f32),
        v((2, rows, wide), f32),
        v((rows, wide), bf16),
        v((rows, wide), bf16),
        v((rows, wide), f32),
        v((NF, NZ, NX, CAP, fc), bf16),
        v((NF, NX, NZ, CAP, fc), bf16),
        v((NZ, NX, CAP, wide), bf16),
        v((NX, NZ, CAP, wide), bf16),
        v((NF, rows, fc), bf16),
        v((NZ, NF, rank, fc), f32),
        v((NZ, NF, rank, fc), bf16),
        v((NZ, NF, rank, fc), bf16),
        v((NZ, NF, rank, fc), bf16),
        v((NZ, rank, wide), bf16),
        v((NZ, rank, wide), bf16),
        dma((NF,)), dma((NF,)),
        dma((NF, NX - 1)), dma((NF, NX - 1)),
        dma((NX - 1,)), dma((NX - 1,)),
        dma((3,)), dma((3,)),
        dma((NZ - 1,)), dma((NZ - 1,)),
        dma((NZ, ND, 2)), dma((NZ, ND)),
        dma((8,)), dma((8,)),
        dma((NF, NX - 1)), dma((NF, NX - 1)),
        dma((NX - 1,)), dma((NX - 1,)),
        dma((NF,)), dma((NF,)),
        dma((NZ, NF)), dma((NZ, NF)), dma((NZ, NF)),
        dma((NZ - 1,)), dma((NZ - 1,)),
    ]
    vm = pl.BlockSpec(memory_space=pltpu.VMEM)
    return pl.pallas_call(
        body,
        out_shape=(
            jax.ShapeDtypeStruct(cotangent.shape, bf16),
            jax.ShapeDtypeStruct(handed.shape, bf16),
            jax.ShapeDtypeStruct(adapt_down.shape, bf16),
            jax.ShapeDtypeStruct(adapt_up.shape, bf16),
        ),
        in_specs=[vm] * 6 + [pl.BlockSpec(memory_space=pltpu.SMEM)],
        out_specs=(vm,) * 4,
        scratch_shapes=scratch,
        compiler_params=pltpu.CompilerParams(
            collective_id=0, has_side_effects=True, vmem_limit_bytes=48 * 2**20
        ),
        name="relay",
    )(handed, cotangent, base_weight, adapt_down, adapt_up, row_jobs, job_ranks)


def solution(mesh):
    return jax.shard_map(
        shards,
        mesh=mesh,
        in_specs=(
            P("pipe", "dp", "tensor"),
            P("pipe", "dp", "tensor"),
            P("pipe", "tensor", None),
            P("pipe", "dp", "tensor", None),
            P("pipe", "dp", None, "tensor"),
            P("pipe", "dp", None),
            P(),
        ),
        out_specs=(
            P("pipe", "dp", "tensor"),
            P("pipe", "dp", "tensor"),
            P("pipe", "dp", "tensor", None),
            P("pipe", "dp", None, "tensor"),
        ),
        check_vma=False,
    )
```

```python
import functools

import jax
import jax.numpy as jnp
from jax import lax
from jax.experimental import pallas as pl
from jax.experimental.pallas import tpu as pltpu
from jax.sharding import PartitionSpec as P

ALPHA = 4.0
NX = 4
NZ = 4
CAP = 32
NF = 8
ND = 4
GP = 2
GL = 2
RS0 = 3
RL = 2
N0 = 7
XB = 6
YB = 8
LW0 = 9
LW = tuple(LW0 + ND - 1 + k for k in (0, 1, 3, 4, 5))
BO = (NF, NF + 1, NF + 3)
YL = 8
STEPS = max(LW[4] + 1, N0 + NF + RL, YB + NF)
VMEM = 61 * 2**20
f32, bf16 = jnp.float32, jnp.bfloat16


def nn(a, b):
    return jnp.dot(a, b, preferred_element_type=f32)


def nt(a, b):
    return lax.dot_general(a, b, (((1,), (1,)), ((), ())), preferred_element_type=f32)


def tn(a, b):
    return lax.dot_general(a, b, (((0,), (0,)), ((), ())), preferred_element_type=f32)


def body(
    handed, cot, weight_in, down, up, jobs_in, ranks_in,
    proj, igrad, dgrad, ugrad,
    weight, cotv, jobs, ranks, projv, dgv, ugv,
    inp, to_slots, to_rows, xs, xr, cs, cr, cotf, up4, dn4,
    lgp, lgx, lgs, lgz, lg, lgt,
    lwp, lwx, lws, lwz, lw,
    bo, box, bos, boz, base,
    bs, br, los, lor, ybs,
    own, sp, rl, rr, ugs, ugr,
    y_s, y_r, x_s, x_r, c_s, c_r, ct_s, ct_r, up_s, up_r, dn_s, dn_r,
    ex_s, ex_r, b_s, b_r, lo_s, lo_r, yb_s, yb_r, rs_s, rl_r, rr_r, ug_s, ug_r, in_s, out_s,
):
    rows = inp.shape[1]
    fc = inp.shape[2]
    dc = dn4.shape[1] // ND
    wide = up.shape[3]
    npipe = lax.axis_size("pipe")
    p, d, t = lax.axis_index("pipe"), lax.axis_index("dp"), lax.axis_index("tensor")
    x, z = d // NZ, d % NZ
    c = t % 2
    h = t // 2
    after = {"pipe": (p + 1) % npipe}
    before = {"pipe": (p + npipe - 1) % npipe}
    x_peer = [{"dp": ((x + i) % NX) * NZ + z} for i in range(1, NX)]
    z_peer = [{"dp": x * NZ + (z + i) % NZ} for i in range(1, NZ)]
    z_up = {"dp": x * NZ + jnp.minimum(z + 1, NZ - 1)}
    z_dn = {"dp": x * NZ + jnp.maximum(z - 1, 0)}
    twin = {"tensor": t + 1 - 2 * c}
    far = {"tensor": (t + 2) % 4}

    def remote(src, dst, s, r, who):
        return pltpu.make_async_remote_copy(
            src_ref=src, dst_ref=dst, send_sem=s, recv_sem=r,
            device_id=who, device_id_type=pl.DeviceIdType.MESH,
        )

    bar = pltpu.get_barrier_semaphore()
    everyone = [after, before, twin, far] + x_peer + z_peer
    for who in everyone:
        pl.semaphore_signal(bar, inc=1, device_id=who, device_id_type=pl.DeviceIdType.MESH)

    cot_lanes = pl.ds(pl.multiple_of(t * wide, wide), wide)
    loads = [
        pltpu.make_async_copy(src, dst, in_s.at[k])
        for k, (src, dst) in enumerate([
            (jobs_in, jobs), (ranks_in, ranks), (cot.at[0], cotv), (up.at[0, 0], up4.at[z]),
            (down.at[0, 0], dn4.at[z]), (cot.at[0], cotf.at[:, cot_lanes]),
            (weight_in.at[0], weight),
        ])
    ]
    for one in loads:
        one.start()
    loads[0].wait()

    mine = jobs[...]
    hot = (mine == lax.broadcasted_iota(jnp.int32, (16, rows), 0)).astype(f32).astype(bf16)
    same = tn(hot, hot)
    i0 = lax.broadcasted_iota(jnp.int32, (rows, rows), 0)
    i1 = lax.broadcasted_iota(jnp.int32, (rows, rows), 1)
    rank_col = jnp.sum(jnp.where(i1 < i0, same, 0.0), axis=1, keepdims=True)
    rank_row = jnp.sum(jnp.where(i0 < i1, same, 0.0), axis=0, keepdims=True)
    slot_row = mine.astype(f32) * CAP + rank_row
    numbers = lax.broadcasted_iota(jnp.int32, (16, 128), 0).astype(f32).astype(bf16)
    slot_col = tn(hot, numbers)[:, 0:1] * CAP + rank_col
    slots = to_slots.shape[0]
    to_rows[...] = (
        lax.broadcasted_iota(jnp.int32, (rows, slots), 1).astype(f32) == slot_col
    ).astype(f32).astype(bf16)
    to_slots[...] = (
        lax.broadcasted_iota(jnp.int32, (slots, rows), 0).astype(f32) == slot_row
    ).astype(f32).astype(bf16)

    def y_copy(f):
        return remote(
            handed.at[0, :, pl.ds(pl.multiple_of(f * fc, fc), fc)], inp.at[f],
            y_s.at[f], y_r.at[f], after,
        )

    def c_copy(i):
        return remote(
            cs.at[(x + i) % NX], cr.at[:, x], c_s.at[i - 1], c_r.at[i - 1], x_peer[i - 1]
        )

    def x_copy(f, i):
        return remote(
            xs.at[f, (x + i) % NX], xr.at[f, :, x], x_s.at[f, i - 1], x_r.at[f, i - 1],
            x_peer[i - 1],
        )

    def b_copy(f, i):
        return remote(
            bs.at[f, :, (x + i) % NX], br.at[f, x], b_s.at[f, i - 1], b_r.at[f, i - 1],
            x_peer[i - 1],
        )

    def lo_copy(i):
        return remote(
            los.at[:, (x + i) % NX], lor.at[x], lo_s.at[i - 1], lo_r.at[i - 1],
            x_peer[i - 1],
        )

    def up_copy(i):
        return remote(up4.at[z], up4.at[z], up_s.at[i - 1], up_r.at[i - 1], z_peer[i - 1])

    def ug_copy(i):
        return remote(
            ugs.at[(z + i) % NZ], ugr.at[z], ug_s.at[i - 1], ug_r.at[i - 1], z_peer[i - 1]
        )

    lanes_of = lambda k: cotf.at[:, pl.ds(pl.multiple_of(k * wide, wide), wide)]
    cot_twin = remote(cot.at[0], lanes_of(t), ct_s.at[0], ct_r.at[0], twin)
    cot_far = remote(cot.at[0], lanes_of(t), ct_s.at[1], ct_r.at[1], far)
    cot_on = remote(
        lanes_of((t + 2) % 4), lanes_of((t + 2) % 4), ct_s.at[2], ct_r.at[2], twin
    )

    def dn_part(o, f):
        return dn4.at[o, pl.ds(pl.multiple_of(f * dc, dc), dc)]

    def next_dn(o, f, way):
        who, k = (z_up, 0) if way > 0 else (z_dn, 1)
        return remote(dn_part(o, f), dn_part(o, f), dn_s.at[o, f, k], dn_r.at[o, f], who)

    half = lg.shape[0] // 2
    here, there = pl.multiple_of(c * half, half), pl.multiple_of((1 - c) * half, half)
    lg_twin = remote(lgp.at[pl.ds(there, half)], lgx, ex_s.at[0], ex_r.at[0], twin)
    lg_far = remote(lgs, lgz, ex_s.at[1], ex_r.at[1], far)
    lg_swap = remote(
        lg.at[pl.ds(here, half)], lg.at[pl.ds(here, half)], ex_s.at[2], ex_r.at[2], twin
    )
    lw_twin = remote(lwp.at[pl.ds(there, half)], lwx, ex_s.at[3], ex_r.at[3], twin)
    lw_far = remote(lws, lwz, ex_s.at[4], ex_r.at[4], far)
    lw_swap = remote(
        lw.at[pl.ds(here, half)], lw.at[pl.ds(here, half)], ex_s.at[5], ex_r.at[5], twin
    )
    bo_twin = remote(bo.at[1 - c], box, ex_s.at[6], ex_r.at[6], twin)
    bo_far = remote(bos, boz, ex_s.at[7], ex_r.at[7], far)

    def yb_copy(f):
        return remote(
            ybs.at[f], igrad.at[0, :, pl.ds(pl.multiple_of(f * fc, fc), fc)],
            yb_s.at[f], yb_r.at[f], before,
        )

    def rs_up(o, f):
        return remote(sp.at[o, f], rl.at[o, f], rs_s.at[o, f], rl_r.at[o, f], z_up)

    def rs_dn(o, f):
        return remote(sp.at[o, f], rr.at[o, f], rs_s.at[o, f], rr_r.at[o, f], z_dn)

    def dg_out(f):
        at = pl.ds(pl.multiple_of(f * fc, fc), fc)
        return pltpu.make_async_copy(dgv.at[f], dgrad.at[0, 0, at], out_s.at[f])

    proj_out = pltpu.make_async_copy(projv, proj.at[0], out_s.at[NF])
    ug_out = pltpu.make_async_copy(ugv, ugrad.at[0, 0], out_s.at[NF + 1])

    def each(count, fn):
        def go(i, carry):
            fn(i)
            return carry

        lax.fori_loop(0, count, go, 0)

    for one in loads[1:5]:
        one.wait()
    for j in range(NX):
        got = nn(to_slots[j * 128 : (j + 1) * 128], cotv[...]).astype(bf16)
        cs[j] = got.reshape(NZ, CAP, wide)

    pl.semaphore_wait(bar, len(everyone))

    for i in range(1, NX):
        c_copy(i).start()
    y_copy(0).start()
    for i in range(1, NZ):
        up_copy(i).start()
    cot_far.start()
    cot_twin.start()
    each(YL - 1, lambda f: y_copy(f + 1).start())
    for k in range(NZ):
        cr[k, x] = cs[x, k]

    @pl.when(z == 0)
    def _():
        each(ND, lambda f: next_dn(0, f, 1).start())

    @pl.when(z == NZ - 1)
    def _():
        each(ND, lambda f: next_dn(NZ - 1, f, -1).start())

    for one in loads[5:]:
        one.wait()
    bo[...] = jnp.zeros_like(bo)
    lwp[...] = jnp.zeros_like(lwp)

    def factor_of(k):
        rank = ranks[x * NZ + k]
        lane = lax.broadcasted_iota(jnp.int32, (1, 128), 1)
        many = jnp.full((1, 128), rank, jnp.int32)
        return jnp.where(lane < many, ALPHA / jnp.sqrt(many.astype(f32)), 0.0)

    def step(s, carry):
        @pl.when(s < NF)
        def _():
            f = s

            @pl.when(f + YL < NF)
            def _():
                y_copy(f + YL).start()

            y_copy(f).wait_recv()
            block = inp[f]
            for j in range(NX):
                got = nn(to_slots[j * 128 : (j + 1) * 128], block).astype(bf16)
                xs[f, j] = got.reshape(NZ, CAP, fc)
            for i in range(1, NX):
                x_copy(f, i).start()
            for k in range(NZ):
                xr[f, k, x] = xs[f, x, k]
            part = nn(block, weight[pl.ds(pl.multiple_of(f * fc, fc), fc)])
            for k in range(4):
                bo[k % 2, k // 2] += part[:, k * wide : (k + 1) * wide]

        @pl.when((s % GP == 0) & (s < GP * ND))
        def _():
            @pl.when((z > 0) & (z < NZ - 1))
            def _():
                next_dn(z, s // GP, 1).start()
                next_dn(z, s // GP, -1).start()

        for o in range(NZ):
            dist = jnp.abs(z - o)
            g = s - GL * dist
            f = g // GP

            @pl.when((dist > 0) & (g >= 0) & (g % GP == 0) & (g < GP * ND))
            def _():
                next_dn(o, f, 1).wait_recv()

                @pl.when((z > o) & (z < NZ - 1))
                def _():
                    next_dn(o, f, 1).start()

                @pl.when((z < o) & (z > 0))
                def _():
                    next_dn(o, f, -1).start()

        @pl.when(s == 0)
        def _():
            cot_far.wait_recv()
            cot_on.start()
            for i in range(1, NX):
                c_copy(i).wait_recv()
            for i in range(1, NZ):
                up_copy(i).wait_recv()
            for k in range(NZ):
                lgp[k * 128 : (k + 1) * 128] = nt(cr[k].reshape(128, wide), up4[k])
            lg_twin.start()

        @pl.when(s == 1)
        def _():
            lg_twin.wait_recv()
            lgx[...] += lgp[pl.ds(here, half)]
            lgs[...] = lgx[...].astype(lgs.dtype)
            lg_far.start()

        @pl.when(s == 2)
        def _():
            lg_far.wait_recv()
            total = lgx[...] + lgz[...].astype(f32)
            for k in range(2):
                lg[pl.ds(pl.multiple_of(c * half + k * 128, 128), 128)] = (
                    total[k * 128 : (k + 1) * 128] * factor_of(2 * c + k)
                ).astype(bf16)
            lg_swap.start()
            cot_twin.wait_recv()
            cot_on.wait_recv()

        @pl.when(s == RS0)
        def _():
            lg_swap.wait_recv()
            for k in range(NZ):
                lgt[k] = lg[k * 128 : (k + 1) * 128].T

        @pl.when((s >= RS0) & (s < RS0 + NF))
        def _():
            f = s - RS0
            for i in range(1, NX):
                x_copy(f, i).wait_recv()
            for k in range(NZ):
                own[k, f] = nn(lgt[k], xr[f, k].reshape(128, fc))

        def pass_up(o, f):
            @pl.when(z == 0)
            def _():
                sp[o, f] = own[o, f].astype(bf16)

            @pl.when(z > 0)
            def _():
                rs_up(o, f).wait_recv()
                sp[o, f] = (own[o, f] + rl[o, f].astype(f32)).astype(bf16)

            rs_up(o, f).start()

        def pass_down(o, f):
            @pl.when(z == NZ - 1)
            def _():
                sp[o, f] = own[o, f].astype(bf16)

            @pl.when(z < NZ - 1)
            def _():
                rs_dn(o, f).wait_recv()
                sp[o, f] = (own[o, f] + rr[o, f].astype(f32)).astype(bf16)

            rs_dn(o, f).start()

        fu = s - RS0 - RL * z
        fd = s - RS0 - RL * (NZ - 1 - z)
        fn = s - N0

        for o in range(NZ - 1, 1, -1):

            @pl.when((fu >= 0) & (fu < NF) & (o > z + 1))
            def _():
                pass_up(o, fu)

        for o in range(NZ - 2):

            @pl.when((fd >= 0) & (fd < NF) & (o < z - 1))
            def _():
                pass_down(o, fd)

        @pl.when((fn >= 0) & (fn < NF) & (z < NZ - 1))
        def _():
            pass_up(z + 1, fn)

        @pl.when((fn >= 0) & (fn < NF) & (z > 0))
        def _():
            pass_down(z - 1, fn)

        fe = s - N0 - RL

        @pl.when((fe >= 0) & (fe < NF))
        def _():
            @pl.when(z > 0)
            def _():
                rs_up(z, fe).wait_recv()
                own[z, fe] += rl[z, fe].astype(f32)

            @pl.when(z < NZ - 1)
            def _():
                rs_dn(z, fe).wait_recv()
                own[z, fe] += rr[z, fe].astype(f32)

            dgv[fe] = own[z, fe].T.astype(bf16)
            dg_out(fe).start()

        @pl.when((s >= XB) & (s < XB + NF))
        def _():
            f = s - XB
            at = pl.ds(pl.multiple_of(f * fc, fc), fc)
            for k in range(NZ):
                back = nt(lg[k * 128 : (k + 1) * 128], dn4[k, at]).astype(bf16)
                bs[f, k] = back.reshape(NX, CAP, fc)
            for i in range(1, NX):
                b_copy(f, i).start()
            for k in range(NZ):
                br[f, x, k] = bs[f, k, x]

        @pl.when((s >= LW0) & (s < LW0 + ND))
        def _():
            for i in range(NF // ND):
                f = (s - LW0) * (NF // ND) + i
                at = pl.ds(pl.multiple_of(f * fc, fc), fc)
                for k in range(NZ):
                    term = nn(xr[f, k].reshape(128, fc), dn4[k, at])
                    lwp[k * 128 : (k + 1) * 128] += term

        @pl.when(s == BO[0])
        def _():
            bo_twin.start()

        @pl.when(s == BO[1])
        def _():
            bo_twin.wait_recv()
            base[...] = bo[c, h] + box[h]
            bos[...] = (bo[c, 1 - h] + box[1 - h]).astype(bos.dtype)
            bo_far.start()

        @pl.when(s == BO[2])
        def _():
            bo_far.wait_recv()
            base[...] += boz[...].astype(f32)

        @pl.when((s >= YB) & (s < YB + NF))
        def _():
            f = s - YB
            part = nt(cotf[...], weight[pl.ds(pl.multiple_of(f * fc, fc), fc)])
            for i in range(1, NX):
                b_copy(f, i).wait_recv()
            ybs[f] = (part + nn(to_rows[...], br[f].reshape(slots, fc))).astype(bf16)
            yb_copy(f).start()

        @pl.when(s == LW[0])
        def _():
            lw_twin.start()

        @pl.when(s == LW[1])
        def _():
            lw_twin.wait_recv()
            lwx[...] += lwp[pl.ds(here, half)]
            lws[...] = lwx[...].astype(lws.dtype)
            lw_far.start()

        @pl.when(s == LW[2])
        def _():
            lw_far.wait_recv()
            total = lwx[...] + lwz[...].astype(f32)
            for k in range(2):
                lw[pl.ds(pl.multiple_of(c * half + k * 128, 128), 128)] = (
                    total[k * 128 : (k + 1) * 128] * factor_of(2 * c + k)
                ).astype(bf16)
            lw_swap.start()

        @pl.when(s == LW[3])
        def _():
            lw_swap.wait_recv()
            for k in range(NZ):
                low = lw[k * 128 : (k + 1) * 128]
                los[k] = nn(low, up4[k]).astype(bf16).reshape(NX, CAP, wide)
                ugs[k] = tn(low, cr[k].reshape(128, wide)).astype(bf16)
            for i in range(1, NX):
                lo_copy(i).start()
            for i in range(1, NZ):
                ug_copy(i).start()
            for k in range(NZ):
                lor[x, k] = los[k, x]

        @pl.when(s == LW[4])
        def _():
            for i in range(1, NX):
                lo_copy(i).wait_recv()
            projv[...] = (base[...] + nn(to_rows[...], lor[...].reshape(slots, wide))).astype(
                bf16
            )
            proj_out.start()
            ugr[z] = ugs[z]
            for i in range(1, NZ):
                ug_copy(i).wait_recv()
            total = ugr[0].astype(f32)
            for k in range(1, NZ):
                total += ugr[k].astype(f32)
            ugv[...] = total.astype(bf16)
            ug_out.start()

        return carry

    lax.fori_loop(0, STEPS, step, 0)

    for one in (cot_twin, cot_far, cot_on, lg_twin, lg_far, lg_swap, lw_twin, lw_far,
                lw_swap, bo_twin, bo_far):
        one.wait_send()
    for i in range(1, NX):
        c_copy(i).wait_send()
        lo_copy(i).wait_send()
    for i in range(1, NZ):
        up_copy(i).wait_send()
        ug_copy(i).wait_send()

    def last(f):
        y_copy(f).wait_send()
        for i in range(1, NX):
            x_copy(f, i).wait_send()
            b_copy(f, i).wait_send()
        yb_copy(f).wait_send()
        for o in range(NZ):

            @pl.when(o > z)
            def _():
                rs_up(o, f).wait_send()

            @pl.when(o < z)
            def _():
                rs_dn(o, f).wait_send()

    each(NF, last)

    def last_dn(f):
        for o in range(NZ):

            @pl.when((o <= z) & (z < NZ - 1))
            def _():
                next_dn(o, f, 1).wait_send()

            @pl.when((o >= z) & (z > 0))
            def _():
                next_dn(o, f, -1).wait_send()

    each(ND, last_dn)
    each(NF, lambda f: dg_out(f).wait())
    proj_out.wait()
    ug_out.wait()
    each(NF, lambda f: yb_copy(f).wait_recv())


def flush(*refs):
    ins, outs, mids, sems = refs[:4], refs[4:8], refs[8:12], refs[12]
    first = [
        pltpu.make_async_copy(src, mid, sems.at[0, k])
        for k, (src, mid) in enumerate(zip(ins, mids))
    ]
    second = [
        pltpu.make_async_copy(mid, dst, sems.at[1, k])
        for k, (mid, dst) in enumerate(zip(mids, outs))
    ]
    for k in (1, 2, 0, 3):
        first[k].start()
    for k in (1, 2, 0, 3):
        first[k].wait()
        second[k].start()
    for one in second:
        one.wait()


def shards(handed, cotangent, base_weight, adapt_down, adapt_up, row_jobs, job_ranks):
    _, rows, feats = handed.shape
    wide = cotangent.shape[2]
    out = base_weight.shape[2]
    rank = adapt_down.shape[3]
    fc = feats // NF
    slots = NX * NZ * CAP
    lane = NX * CAP
    half = slots // 2
    v = pltpu.VMEM
    dma = pltpu.SemaphoreType.DMA
    scratch = [
        v((feats, out), bf16),
        v((rows, wide), bf16),
        v((1, rows), jnp.int32),
        pltpu.SMEM(job_ranks.shape, jnp.int32),
        v((rows, wide), bf16),
        v((NF, fc, rank), bf16),
        v((rank, wide), bf16),
        v((NF, rows, fc), bf16),
        v((slots, rows), bf16),
        v((rows, slots), bf16),
        v((NF, NX, NZ, CAP, fc), bf16),
        v((NF, NZ, NX, CAP, fc), bf16),
        v((NX, NZ, CAP, wide), bf16),
        v((NZ, NX, CAP, wide), bf16),
        v((rows, out), bf16),
        v((NZ, rank, wide), bf16),
        v((NZ, feats, rank), bf16),
        v((slots, rank), f32),
        v((half, rank), f32),
        v((half, rank), bf16),
        v((half, rank), bf16),
        v((slots, rank), bf16),
        v((NZ, rank, lane), bf16),
        v((slots, rank), f32),
        v((half, rank), f32),
        v((half, rank), bf16),
        v((half, rank), bf16),
        v((slots, rank), bf16),
        v((2, 2, rows, wide), f32),
        v((2, rows, wide), f32),
        v((rows, wide), bf16),
        v((rows, wide), bf16),
        v((rows, wide), f32),
        v((NF, NZ, NX, CAP, fc), bf16),
        v((NF, NX, NZ, CAP, fc), bf16),
        v((NZ, NX, CAP, wide), bf16),
        v((NX, NZ, CAP, wide), bf16),
        v((NF, rows, fc), bf16),
        v((NZ, NF, rank, fc), f32),
        v((NZ, NF, rank, fc), bf16),
        v((NZ, NF, rank, fc), bf16),
        v((NZ, NF, rank, fc), bf16),
        v((NZ, rank, wide), bf16),
        v((NZ, rank, wide), bf16),
        dma((NF,)), dma((NF,)),
        dma((NF, NX - 1)), dma((NF, NX - 1)),
        dma((NX - 1,)), dma((NX - 1,)),
        dma((3,)), dma((3,)),
        dma((NZ - 1,)), dma((NZ - 1,)),
        dma((NZ, ND, 2)), dma((NZ, ND)),
        dma((8,)), dma((8,)),
        dma((NF, NX - 1)), dma((NF, NX - 1)),
        dma((NX - 1,)), dma((NX - 1,)),
        dma((NF,)), dma((NF,)),
        dma((NZ, NF)), dma((NZ, NF)), dma((NZ, NF)),
        dma((NZ - 1,)), dma((NZ - 1,)),
        dma((7,)),
        dma((NF + 2,)),
    ]
    hbm = pl.BlockSpec(memory_space=pltpu.HBM)
    shapes = (
        jax.ShapeDtypeStruct(cotangent.shape, bf16),
        jax.ShapeDtypeStruct(handed.shape, bf16),
        jax.ShapeDtypeStruct(adapt_down.shape, bf16),
        jax.ShapeDtypeStruct(adapt_up.shape, bf16),
    )
    results = pl.pallas_call(
        body,
        out_shape=shapes,
        in_specs=[hbm] * 7,
        out_specs=(hbm,) * 4,
        scratch_shapes=scratch,
        compiler_params=pltpu.CompilerParams(
            collective_id=0, has_side_effects=True, vmem_limit_bytes=VMEM
        ),
        name="relay",
    )(handed, cotangent, base_weight, adapt_down, adapt_up, row_jobs.reshape(1, rows), job_ranks)
    return pl.pallas_call(
        flush,
        out_shape=shapes,
        in_specs=[hbm] * 4,
        out_specs=(hbm,) * 4,
        scratch_shapes=[v(one.shape, one.dtype) for one in shapes] + [dma((2, 4))],
        compiler_params=pltpu.CompilerParams(vmem_limit_bytes=VMEM),
        name="flush",
    )(*results)


def solution(mesh):
    return jax.shard_map(
        shards,
        mesh=mesh,
        in_specs=(
            P("pipe", "dp", "tensor"),
            P("pipe", "dp", "tensor"),
            P("pipe", "tensor", None),
            P("pipe", "dp", "tensor", None),
            P("pipe", "dp", None, "tensor"),
            P("pipe", "dp", None),
            P(),
        ),
        out_specs=(
            P("pipe", "dp", "tensor"),
            P("pipe", "dp", "tensor"),
            P("pipe", "dp", "tensor", None),
            P("pipe", "dp", None, "tensor"),
        ),
        check_vma=False,
    )
```

```python
import functools

import jax
import jax.numpy as jnp
from jax import lax
from jax.experimental import pallas as pl
from jax.experimental.pallas import tpu as pltpu
from jax.sharding import PartitionSpec as P

ALPHA = 4.0
NX = 4
NZ = 4
CAP = 32
NF = 8
ND = 4
GP = 2
GL = 2
RS0 = 3
RL = 2
N0 = 7
XB = 6
YB = 8
LW0 = 9
LW = tuple(LW0 + ND - 1 + k for k in (0, 1, 3, 4, 5))
BO = (11, 12, 14)
YL = 8
END = max(N0, YB) + 2
STEPS = max(LW[4] + 1, N0 + NF + RL, END + NF)
VMEM = 61 * 2**20
f32, bf16 = jnp.float32, jnp.bfloat16


def nn(a, b):
    return jnp.dot(a, b, preferred_element_type=f32)


def nt(a, b):
    return lax.dot_general(a, b, (((1,), (1,)), ((), ())), preferred_element_type=f32)


def tn(a, b):
    return lax.dot_general(a, b, (((0,), (0,)), ((), ())), preferred_element_type=f32)


def body(
    handed, cot, weight_in, down, up, jobs_in, ranks_in,
    proj, igrad, dgrad, ugrad,
    weight, cotv, jobs, ranks, projv, dgv, ugv,
    inp, to_slots, to_rows, xs, xr, cs, cr, cotf, up4, dn4,
    lgp, lgx, lgs, lgz, lg, lgt,
    lwp, lwx, lws, lwz, lw,
    bo, box, bos, boz, base,
    bs, br, los, lor, ybs,
    own, sp, rl, rr, ugs, ugr,
    y_s, y_r, x_s, x_r, c_s, c_r, ct_s, ct_r, up_s, up_r, dn_s, dn_r,
    ex_s, ex_r, b_s, b_r, lo_s, lo_r, yb_s, yb_r, rs_s, rl_r, rr_r, ug_s, ug_r, in_s, out_s,
):
    rows = inp.shape[1]
    fc = inp.shape[2]
    dc = dn4.shape[1] // ND
    wide = up.shape[3]
    npipe = lax.axis_size("pipe")
    p, d, t = lax.axis_index("pipe"), lax.axis_index("dp"), lax.axis_index("tensor")
    x, z = d // NZ, d % NZ
    c = t % 2
    h = t // 2
    after = {"pipe": (p + 1) % npipe}
    before = {"pipe": (p + npipe - 1) % npipe}
    x_peer = [{"dp": ((x + i) % NX) * NZ + z} for i in range(1, NX)]
    z_peer = [{"dp": x * NZ + (z + i) % NZ} for i in range(1, NZ)]
    z_up = {"dp": x * NZ + jnp.minimum(z + 1, NZ - 1)}
    z_dn = {"dp": x * NZ + jnp.maximum(z - 1, 0)}
    twin = {"tensor": t + 1 - 2 * c}
    far = {"tensor": (t + 2) % 4}

    def remote(src, dst, s, r, who):
        return pltpu.make_async_remote_copy(
            src_ref=src, dst_ref=dst, send_sem=s, recv_sem=r,
            device_id=who, device_id_type=pl.DeviceIdType.MESH,
        )

    bar = pltpu.get_barrier_semaphore()
    everyone = [after, before, twin, far] + x_peer + z_peer
    for who in everyone:
        pl.semaphore_signal(bar, inc=1, device_id=who, device_id_type=pl.DeviceIdType.MESH)

    cot_lanes = pl.ds(pl.multiple_of(t * wide, wide), wide)
    loads = [
        pltpu.make_async_copy(src, dst, in_s.at[k])
        for k, (src, dst) in enumerate([
            (jobs_in, jobs), (ranks_in, ranks), (cot.at[0], cotv), (up.at[0, 0], up4.at[z]),
            (down.at[0, 0], dn4.at[z]), (cot.at[0], cotf.at[:, cot_lanes]),
            (weight_in.at[0], weight),
        ])
    ]
    for one in loads:
        one.start()
    slots = to_slots.shape[0]

    def y_copy(f):
        return remote(
            handed.at[0, :, pl.ds(pl.multiple_of(f * fc, fc), fc)], inp.at[f],
            y_s.at[f], y_r.at[f], after,
        )

    def c_copy(i):
        return remote(
            cs.at[(x + i) % NX], cr.at[x], c_s.at[i - 1], c_r.at[i - 1], x_peer[i - 1]
        )

    def x_copy(f, i):
        return remote(
            xs.at[f, (x + i) % NX], xr.at[f, x], x_s.at[f, i - 1], x_r.at[f, i - 1],
            x_peer[i - 1],
        )

    def b_copy(f, i):
        return remote(
            bs.at[f, (x + i) % NX], br.at[f, x], b_s.at[f, i - 1], b_r.at[f, i - 1],
            x_peer[i - 1],
        )

    def lo_copy(i):
        return remote(
            los.at[(x + i) % NX], lor.at[x], lo_s.at[i - 1], lo_r.at[i - 1],
            x_peer[i - 1],
        )

    def up_copy(i):
        return remote(up4.at[z], up4.at[z], up_s.at[i - 1], up_r.at[i - 1], z_peer[i - 1])

    def ug_copy(i):
        return remote(
            ugs.at[(z + i) % NZ], ugr.at[z], ug_s.at[i - 1], ug_r.at[i - 1], z_peer[i - 1]
        )

    lanes_of = lambda k: cotf.at[:, pl.ds(pl.multiple_of(k * wide, wide), wide)]
    cot_twin = remote(cot.at[0], lanes_of(t), ct_s.at[0], ct_r.at[0], twin)
    cot_far = remote(cot.at[0], lanes_of(t), ct_s.at[1], ct_r.at[1], far)
    cot_on = remote(
        lanes_of((t + 2) % 4), lanes_of((t + 2) % 4), ct_s.at[2], ct_r.at[2], twin
    )

    def dn_part(o, f):
        return dn4.at[o, pl.ds(pl.multiple_of(f * dc, dc), dc)]

    def next_dn(o, f, way):
        who, k = (z_up, 0) if way > 0 else (z_dn, 1)
        return remote(dn_part(o, f), dn_part(o, f), dn_s.at[o, f, k], dn_r.at[o, f], who)

    half = lg.shape[0] // 2
    here, there = pl.multiple_of(c * half, half), pl.multiple_of((1 - c) * half, half)
    lg_twin = remote(lgp.at[pl.ds(there, half)], lgx, ex_s.at[0], ex_r.at[0], twin)
    lg_far = remote(lgs, lgz, ex_s.at[1], ex_r.at[1], far)
    lg_swap = remote(
        lg.at[pl.ds(here, half)], lg.at[pl.ds(here, half)], ex_s.at[2], ex_r.at[2], twin
    )
    lw_twin = remote(lwp.at[pl.ds(there, half)], lwx, ex_s.at[3], ex_r.at[3], twin)
    lw_far = remote(lws, lwz, ex_s.at[4], ex_r.at[4], far)
    lw_swap = remote(
        lw.at[pl.ds(here, half)], lw.at[pl.ds(here, half)], ex_s.at[5], ex_r.at[5], twin
    )
    bo_twin = remote(bo.at[1 - c], box, ex_s.at[6], ex_r.at[6], twin)
    bo_far = remote(bos, boz, ex_s.at[7], ex_r.at[7], far)

    def yb_copy(f):
        return remote(
            ybs.at[f], igrad.at[0, :, pl.ds(pl.multiple_of(f * fc, fc), fc)],
            yb_s.at[f], yb_r.at[f], before,
        )

    def rs_up(o, f):
        return remote(sp.at[o, f], rl.at[o, f], rs_s.at[o, f], rl_r.at[o, f], z_up)

    def rs_dn(o, f):
        return remote(sp.at[o, f], rr.at[o, f], rs_s.at[o, f], rr_r.at[o, f], z_dn)

    def dg_out(f):
        at = pl.ds(pl.multiple_of(f * fc, fc), fc)
        return pltpu.make_async_copy(dgv.at[f], dgrad.at[0, 0, at], out_s.at[f])

    proj_out = pltpu.make_async_copy(projv, proj.at[0], out_s.at[NF])
    ug_out = pltpu.make_async_copy(ugv, ugrad.at[0, 0], out_s.at[NF + 1])

    def each(count, fn):
        def go(i, carry):
            fn(i)
            return carry

        lax.fori_loop(0, count, go, 0)

    pl.semaphore_wait(bar, len(everyone))

    y_copy(0).start()
    cot_far.start()
    cot_twin.start()
    each(YL - 1, lambda f: y_copy(f + 1).start())
    for one in loads[1:5]:
        one.wait()
    for i in range(1, NZ):
        up_copy(i).start()

    @pl.when(z == 0)
    def _():
        each(ND, lambda f: next_dn(0, f, 1).start())

    @pl.when(z == NZ - 1)
    def _():
        each(ND, lambda f: next_dn(NZ - 1, f, -1).start())

    loads[0].wait()

    mine = jobs[...]
    hot = (mine == lax.broadcasted_iota(jnp.int32, (16, rows), 0)).astype(f32).astype(bf16)
    same = tn(hot, hot)
    i0 = lax.broadcasted_iota(jnp.int32, (rows, rows), 0)
    i1 = lax.broadcasted_iota(jnp.int32, (rows, rows), 1)
    rank_col = jnp.sum(jnp.where(i1 < i0, same, 0.0), axis=1, keepdims=True)
    rank_row = jnp.sum(jnp.where(i0 < i1, same, 0.0), axis=0, keepdims=True)
    slot_row = mine.astype(f32) * CAP + rank_row
    numbers = lax.broadcasted_iota(jnp.int32, (16, 128), 0).astype(f32).astype(bf16)
    slot_col = tn(hot, numbers)[:, 0:1] * CAP + rank_col
    to_rows[...] = (
        lax.broadcasted_iota(jnp.int32, (rows, slots), 1).astype(f32) == slot_col
    ).astype(f32).astype(bf16)
    to_slots[...] = (
        lax.broadcasted_iota(jnp.int32, (slots, rows), 0).astype(f32) == slot_row
    ).astype(f32).astype(bf16)
    for j in range(NX):
        got = nn(to_slots[j * 128 : (j + 1) * 128], cotv[...]).astype(bf16)
        cs[j] = got.reshape(NZ, CAP, wide)
    for i in range(1, NX):
        c_copy(i).start()
    cr[x] = cs[x]

    for one in loads[5:]:
        one.wait()
    bo[...] = jnp.zeros_like(bo)
    lwp[...] = jnp.zeros_like(lwp)

    def factor_of(k):
        rank = ranks[x * NZ + k]
        lane = lax.broadcasted_iota(jnp.int32, (1, 128), 1)
        many = jnp.full((1, 128), rank, jnp.int32)
        return jnp.where(lane < many, ALPHA / jnp.sqrt(many.astype(f32)), 0.0)

    def last(f):
        y_copy(f).wait_send()
        for i in range(1, NX):
            x_copy(f, i).wait_send()
            b_copy(f, i).wait_send()
        yb_copy(f).wait_send()
        for o in range(NZ):

            @pl.when(o > z)
            def _():
                rs_up(o, f).wait_send()

            @pl.when(o < z)
            def _():
                rs_dn(o, f).wait_send()

    def step(s, carry):
        @pl.when(s < NF)
        def _():
            f = s

            @pl.when(f + YL < NF)
            def _():
                y_copy(f + YL).start()

            y_copy(f).wait_recv()
            block = inp[f]
            for j in range(NX):
                got = nn(to_slots[j * 128 : (j + 1) * 128], block).astype(bf16)
                xs[f, j] = got.reshape(NZ, CAP, fc)
            for i in range(1, NX):
                x_copy(f, i).start()
            xr[f, x] = xs[f, x]
            part = nn(block, weight[pl.ds(pl.multiple_of(f * fc, fc), fc)])
            for k in range(4):
                bo[k % 2, k // 2] += part[:, k * wide : (k + 1) * wide]

        @pl.when((s % GP == 0) & (s < GP * ND))
        def _():
            @pl.when((z > 0) & (z < NZ - 1))
            def _():
                next_dn(z, s // GP, 1).start()
                next_dn(z, s // GP, -1).start()

        for o in range(NZ):
            dist = jnp.abs(z - o)
            g = s - GL * dist
            f = g // GP

            @pl.when((dist > 0) & (g >= 0) & (g % GP == 0) & (g < GP * ND))
            def _():
                next_dn(o, f, 1).wait_recv()

                @pl.when((z > o) & (z < NZ - 1))
                def _():
                    next_dn(o, f, 1).start()

                @pl.when((z < o) & (z > 0))
                def _():
                    next_dn(o, f, -1).start()

        @pl.when(s == 0)
        def _():
            cot_far.wait_recv()
            cot_on.start()
            for i in range(1, NX):
                c_copy(i).wait_recv()
            for i in range(1, NZ):
                up_copy(i).wait_recv()
            for k in range(NZ):
                lgp[k * 128 : (k + 1) * 128] = nt(cr[:, k].reshape(128, wide), up4[k])
            lg_twin.start()

        @pl.when(s == 1)
        def _():
            lg_twin.wait_recv()
            lgx[...] += lgp[pl.ds(here, half)]
            lgs[...] = lgx[...].astype(lgs.dtype)
            lg_far.start()

        @pl.when(s == 2)
        def _():
            lg_far.wait_recv()
            total = lgx[...] + lgz[...].astype(f32)
            for k in range(2):
                lg[pl.ds(pl.multiple_of(c * half + k * 128, 128), 128)] = (
                    total[k * 128 : (k + 1) * 128] * factor_of(2 * c + k)
                ).astype(bf16)
            lg_swap.start()
            cot_twin.wait_recv()
            cot_on.wait_recv()

        @pl.when(s == RS0)
        def _():
            lg_swap.wait_recv()
            for k in range(NZ):
                lgt[k] = lg[k * 128 : (k + 1) * 128].T

        @pl.when((s >= RS0) & (s < RS0 + NF))
        def _():
            f = s - RS0
            for i in range(1, NX):
                x_copy(f, i).wait_recv()
            for k in range(NZ):
                own[k, f] = nn(lgt[k], xr[f, :, k].reshape(128, fc))

        def pass_up(o, f):
            @pl.when(z == 0)
            def _():
                sp[o, f] = own[o, f].astype(bf16)

            @pl.when(z > 0)
            def _():
                rs_up(o, f).wait_recv()
                sp[o, f] = (own[o, f] + rl[o, f].astype(f32)).astype(bf16)

            rs_up(o, f).start()

        def pass_down(o, f):
            @pl.when(z == NZ - 1)
            def _():
                sp[o, f] = own[o, f].astype(bf16)

            @pl.when(z < NZ - 1)
            def _():
                rs_dn(o, f).wait_recv()
                sp[o, f] = (own[o, f] + rr[o, f].astype(f32)).astype(bf16)

            rs_dn(o, f).start()

        fu = s - RS0 - RL * z
        fd = s - RS0 - RL * (NZ - 1 - z)
        fn = s - N0

        for o in range(NZ - 1, 1, -1):

            @pl.when((fu >= 0) & (fu < NF) & (o > z + 1))
            def _():
                pass_up(o, fu)

        for o in range(NZ - 2):

            @pl.when((fd >= 0) & (fd < NF) & (o < z - 1))
            def _():
                pass_down(o, fd)

        @pl.when((fn >= 0) & (fn < NF) & (z < NZ - 1))
        def _():
            pass_up(z + 1, fn)

        @pl.when((fn >= 0) & (fn < NF) & (z > 0))
        def _():
            pass_down(z - 1, fn)

        fe = s - N0 - RL

        @pl.when((fe >= 0) & (fe < NF))
        def _():
            @pl.when(z > 0)
            def _():
                rs_up(z, fe).wait_recv()
                own[z, fe] += rl[z, fe].astype(f32)

            @pl.when(z < NZ - 1)
            def _():
                rs_dn(z, fe).wait_recv()
                own[z, fe] += rr[z, fe].astype(f32)

            dgv[fe] = own[z, fe].T.astype(bf16)
            dg_out(fe).start()

        @pl.when((s >= XB) & (s < XB + NF))
        def _():
            f = s - XB
            at = pl.ds(pl.multiple_of(f * fc, fc), fc)
            for k in range(NZ):
                back = nt(lg[k * 128 : (k + 1) * 128], dn4[k, at]).astype(bf16)
                bs[f, :, k] = back.reshape(NX, CAP, fc)
            for i in range(1, NX):
                b_copy(f, i).start()
            br[f, x] = bs[f, x]

        @pl.when((s >= LW0) & (s < LW0 + ND))
        def _():
            for i in range(NF // ND):
                f = (s - LW0) * (NF // ND) + i
                at = pl.ds(pl.multiple_of(f * fc, fc), fc)
                for k in range(NZ):
                    term = nn(xr[f, :, k].reshape(128, fc), dn4[k, at])
                    lwp[k * 128 : (k + 1) * 128] += term

        @pl.when(s == BO[0])
        def _():
            bo_twin.start()

        @pl.when(s == BO[1])
        def _():
            bo_twin.wait_recv()
            base[...] = bo[c, h] + box[h]
            bos[...] = (bo[c, 1 - h] + box[1 - h]).astype(bos.dtype)
            bo_far.start()

        @pl.when(s == BO[2])
        def _():
            bo_far.wait_recv()
            base[...] += boz[...].astype(f32)

        @pl.when((s >= YB) & (s < YB + NF))
        def _():
            f = s - YB
            part = nt(cotf[...], weight[pl.ds(pl.multiple_of(f * fc, fc), fc)])
            for i in range(1, NX):
                b_copy(f, i).wait_recv()
            ybs[f] = (part + nn(to_rows[...], br[f].reshape(slots, fc))).astype(bf16)
            yb_copy(f).start()

        @pl.when(s == LW[0])
        def _():
            lw_twin.start()

        @pl.when(s == LW[1])
        def _():
            lw_twin.wait_recv()
            lwx[...] += lwp[pl.ds(here, half)]
            lws[...] = lwx[...].astype(lws.dtype)
            lw_far.start()

        @pl.when(s == LW[2])
        def _():
            lw_far.wait_recv()
            total = lwx[...] + lwz[...].astype(f32)
            for k in range(2):
                lw[pl.ds(pl.multiple_of(c * half + k * 128, 128), 128)] = (
                    total[k * 128 : (k + 1) * 128] * factor_of(2 * c + k)
                ).astype(bf16)
            lw_swap.start()

        @pl.when(s == LW[3])
        def _():
            lw_swap.wait_recv()
            for k in range(NZ):
                low = lw[k * 128 : (k + 1) * 128]
                los[:, k] = nn(low, up4[k]).astype(bf16).reshape(NX, CAP, wide)
                ugs[k] = tn(low, cr[:, k].reshape(128, wide)).astype(bf16)
            for i in range(1, NX):
                lo_copy(i).start()
            for i in range(1, NZ):
                ug_copy(i).start()
            lor[x] = los[x]

        @pl.when(s == LW[4])
        def _():
            for i in range(1, NX):
                lo_copy(i).wait_recv()
            projv[...] = (base[...] + nn(to_rows[...], lor[...].reshape(slots, wide))).astype(
                bf16
            )
            proj_out.start()
            ugr[z] = ugs[z]
            for i in range(1, NZ):
                ug_copy(i).wait_recv()
            total = ugr[0].astype(f32)
            for k in range(1, NZ):
                total += ugr[k].astype(f32)
            ugv[...] = total.astype(bf16)
            ug_out.start()

        @pl.when((s >= END) & (s < END + NF))
        def _():
            last(s - END)

        return carry

    lax.fori_loop(0, STEPS, step, 0)

    for one in (cot_twin, cot_far, cot_on, lg_twin, lg_far, lg_swap, lw_twin, lw_far,
                lw_swap, bo_twin, bo_far):
        one.wait_send()
    for i in range(1, NX):
        c_copy(i).wait_send()
        lo_copy(i).wait_send()
    for i in range(1, NZ):
        up_copy(i).wait_send()
        ug_copy(i).wait_send()


    def last_dn(f):
        for o in range(NZ):

            @pl.when((o <= z) & (z < NZ - 1))
            def _():
                next_dn(o, f, 1).wait_send()

            @pl.when((o >= z) & (z > 0))
            def _():
                next_dn(o, f, -1).wait_send()

    each(ND, last_dn)
    each(NF, lambda f: dg_out(f).wait())
    proj_out.wait()
    ug_out.wait()
    each(NF, lambda f: yb_copy(f).wait_recv())


def flush(*refs):
    ins, outs, mids, sems = refs[:4], refs[4:8], refs[8:12], refs[12]
    first = [
        pltpu.make_async_copy(src, mid, sems.at[0, k])
        for k, (src, mid) in enumerate(zip(ins, mids))
    ]
    second = [
        pltpu.make_async_copy(mid, dst, sems.at[1, k])
        for k, (mid, dst) in enumerate(zip(mids, outs))
    ]
    for k in (1, 2, 0, 3):
        first[k].start()
    for k in (1, 2, 0, 3):
        first[k].wait()
        second[k].start()
    for one in second:
        one.wait()


def shards(handed, cotangent, base_weight, adapt_down, adapt_up, row_jobs, job_ranks):
    _, rows, feats = handed.shape
    wide = cotangent.shape[2]
    out = base_weight.shape[2]
    rank = adapt_down.shape[3]
    fc = feats // NF
    slots = NX * NZ * CAP
    lane = NX * CAP
    half = slots // 2
    v = pltpu.VMEM
    dma = pltpu.SemaphoreType.DMA
    scratch = [
        v((feats, out), bf16),
        v((rows, wide), bf16),
        v((1, rows), jnp.int32),
        pltpu.SMEM(job_ranks.shape, jnp.int32),
        v((rows, wide), bf16),
        v((NF, fc, rank), bf16),
        v((rank, wide), bf16),
        v((NF, rows, fc), bf16),
        v((slots, rows), bf16),
        v((rows, slots), bf16),
        v((NF, NX, NZ, CAP, fc), bf16),
        v((NF, NX, NZ, CAP, fc), bf16),
        v((NX, NZ, CAP, wide), bf16),
        v((NX, NZ, CAP, wide), bf16),
        v((rows, out), bf16),
        v((NZ, rank, wide), bf16),
        v((NZ, feats, rank), bf16),
        v((slots, rank), f32),
        v((half, rank), f32),
        v((half, rank), bf16),
        v((half, rank), bf16),
        v((slots, rank), bf16),
        v((NZ, rank, lane), bf16),
        v((slots, rank), f32),
        v((half, rank), f32),
        v((half, rank), bf16),
        v((half, rank), bf16),
        v((slots, rank), bf16),
        v((2, 2, rows, wide), f32),
        v((2, rows, wide), f32),
        v((rows, wide), bf16),
        v((rows, wide), bf16),
        v((rows, wide), f32),
        v((NF, NX, NZ, CAP, fc), bf16),
        v((NF, NX, NZ, CAP, fc), bf16),
        v((NX, NZ, CAP, wide), bf16),
        v((NX, NZ, CAP, wide), bf16),
        v((NF, rows, fc), bf16),
        v((NZ, NF, rank, fc), f32),
        v((NZ, NF, rank, fc), bf16),
        v((NZ, NF, rank, fc), bf16),
        v((NZ, NF, rank, fc), bf16),
        v((NZ, rank, wide), bf16),
        v((NZ, rank, wide), bf16),
        dma((NF,)), dma((NF,)),
        dma((NF, NX - 1)), dma((NF, NX - 1)),
        dma((NX - 1,)), dma((NX - 1,)),
        dma((3,)), dma((3,)),
        dma((NZ - 1,)), dma((NZ - 1,)),
        dma((NZ, ND, 2)), dma((NZ, ND)),
        dma((8,)), dma((8,)),
        dma((NF, NX - 1)), dma((NF, NX - 1)),
        dma((NX - 1,)), dma((NX - 1,)),
        dma((NF,)), dma((NF,)),
        dma((NZ, NF)), dma((NZ, NF)), dma((NZ, NF)),
        dma((NZ - 1,)), dma((NZ - 1,)),
        dma((7,)),
        dma((NF + 2,)),
    ]
    hbm = pl.BlockSpec(memory_space=pltpu.HBM)
    shapes = (
        jax.ShapeDtypeStruct(cotangent.shape, bf16),
        jax.ShapeDtypeStruct(handed.shape, bf16),
        jax.ShapeDtypeStruct(adapt_down.shape, bf16),
        jax.ShapeDtypeStruct(adapt_up.shape, bf16),
    )
    results = pl.pallas_call(
        body,
        out_shape=shapes,
        in_specs=[hbm] * 7,
        out_specs=(hbm,) * 4,
        scratch_shapes=scratch,
        compiler_params=pltpu.CompilerParams(
            collective_id=0, has_side_effects=True, vmem_limit_bytes=VMEM
        ),
        name="relay",
    )(handed, cotangent, base_weight, adapt_down, adapt_up, row_jobs.reshape(1, rows), job_ranks)
    return pl.pallas_call(
        flush,
        out_shape=shapes,
        in_specs=[hbm] * 4,
        out_specs=(hbm,) * 4,
        scratch_shapes=[v(one.shape, one.dtype) for one in shapes] + [dma((2, 4))],
        compiler_params=pltpu.CompilerParams(vmem_limit_bytes=VMEM),
        name="flush",
    )(*results)


def solution(mesh):
    return jax.shard_map(
        shards,
        mesh=mesh,
        in_specs=(
            P("pipe", "dp", "tensor"),
            P("pipe", "dp", "tensor"),
            P("pipe", "tensor", None),
            P("pipe", "dp", "tensor", None),
            P("pipe", "dp", None, "tensor"),
            P("pipe", "dp", None),
            P(),
        ),
        out_specs=(
            P("pipe", "dp", "tensor"),
            P("pipe", "dp", "tensor"),
            P("pipe", "dp", "tensor", None),
            P("pipe", "dp", None, "tensor"),
        ),
        check_vma=False,
    )
```
